512 devices in a mesh: slab: 128 (over x_lo, z, y), rep: 4 (over x_hi, core).
Axes of the slice: x: 4 (x_hi: 2, x_lo: 2; x = x_hi * 2 + x_lo), y: 8, z: 8, core: 2. Of those that a mesh axis runs over, the one named last changes fastest.
Arguments:
- saved_input: bfloat16 [4, 6, 1, 256, 256, 256], P('rep', None, None, 'slab'), may hold values from -6 to 6
- output_grad: bfloat16 [4, 6, 1, 256, 256, 256], P('rep', None, None, 'slab'), may hold values from -6 to 6
- spectral_weight: float32 [1024, 8, 1, 1, 32], P('slab'), may hold values from -18 to 18
- bypass_weight: float32 [8, 1, 1], replicated, may hold values from -1.8 to 1.8
Outputs:
- input_grad: bfloat16 [4, 6, 1, 256, 256, 256], P('rep', None, None, 'slab')
- weight_grad: float32 [1024, 8, 1, 1, 32], P('slab')
The draws below stay inside these ranges and needn't reach their ends.
All inputs are finite; a program needn't handle non-finite values.
Results may differ from the reference program's by a relative error of at most 0.001.
Values sent between devices are 32-bit elements; how exact they have to be, the bound alone decides.
No kernel may reach another device: no remote copies, remote signals or barrier semaphores. Data moves between devices by JAX's collectives and lax.ppermute only.
A program may use at most 64 MiB of HBM per device.

```python
import jax
import jax.numpy as jnp

NX = 256
NY = 256
NZ = 256
KM = 32
CH = 1
SAMPLES = 4


def block_scale(rng, dims, split, low, top_value):
    level, own = 1.0, jax.random.fold_in(rng, 6)
    for dim, parts in split:
        heights = jnp.exp(jax.random.uniform(jax.random.fold_in(own, dim), (parts,), jnp.float32, low / len(split), top_value / len(split)))
        level = level * jnp.repeat(heights, dims[dim] // parts).reshape([-1 if axis == dim else 1 for axis in range(len(dims))])
    return level


def centred(rng, extent, width, most, cuts=(), kind=jnp.bfloat16):
    drawn = jax.random.normal(rng, extent, jnp.float32) * width
    if len(cuts) > 0:
        drawn = block_scale(rng, extent, cuts, -0.22, 0.18) * drawn
    return jnp.clip(drawn, min=-most, max=most).astype(kind)


def setup_inputs(seed: int = 0) -> dict:
    streams_of = jax.random.split(jax.random.key(seed), 5)
    return {
        "saved_input": centred(streams_of[0], (SAMPLES, 6, CH, NZ, NX, NY), 1.0, 6.0, ((0, 4), (3, 128))),
        "output_grad": centred(streams_of[1], (SAMPLES, 6, CH, NZ, NX, NY), 1.0, 6.0, ((0, 4), (3, 128))),
        "spectral_weight": centred(streams_of[2], (KM * KM, 8, CH, CH, KM), 3.0, 18.0, ((0, 128),), jnp.float32),
        "bypass_weight": centred(streams_of[3], (8, CH, CH), 0.3, 1.8, (), jnp.float32),
    }


def kept(length):
    counter = jnp.arange(KM)
    return jnp.where(counter < KM // 2, counter, length - KM + counter)


def to_complex(field):
    widened = field.astype(jnp.float32)
    return widened[:3] + 1j * widened[3:]


def forward_modes(field):
    spectrum = jnp.fft.fftn(to_complex(field), axes=(2, 3, 4), norm="ortho")
    spectrum = spectrum[:, :, kept(NZ)][:, :, :, kept(NX)][:, :, :, :, kept(NY)]
    return jnp.transpose(spectrum, (3, 4, 0, 1, 2)).reshape(KM * KM, 3, CH, KM)


def reference(saved_input, output_grad, spectral_weight, bypass_weight):
    w_scalar = spectral_weight[:, 0] + 1j * spectral_weight[:, 4]
    w_vector = spectral_weight[:, 1:4] + 1j * spectral_weight[:, 5:8]
    b_scalar = bypass_weight[0] + 1j * bypass_weight[4]
    b_vector = bypass_weight[1:4] + 1j * bypass_weight[5:8]
    depth_index = kept(NZ)[:, None, None]
    first_index = kept(NX)[None, :, None]
    second_index = kept(NY)[None, None, :]
    scalar_grad = jnp.zeros((KM * KM, CH, CH, KM), jnp.float32)
    vector_grad = jnp.zeros((KM * KM, 3, CH, CH, KM), jnp.float32)
    outputs = []
    for sample in range(SAMPLES):
        inputs = forward_modes(saved_input[sample])
        grads = forward_modes(output_grad[sample])
        scalar_grad = scalar_grad + jnp.einsum("rkim,rkom->roim", jnp.conj(inputs), grads)
        vector_grad = vector_grad - 1j * jnp.cross(jnp.conj(inputs)[:, :, None, :, :], grads[:, :, :, None, :], axis=1)
        mode_grads = jnp.einsum("roim,rkom->rkim", jnp.conj(w_scalar), grads)
        mode_grads = mode_grads + 1j * jnp.sum(jnp.cross(jnp.conj(w_vector), grads[:, :, :, None, :], axis=1), axis=2)
        cube = jnp.transpose(mode_grads.reshape(KM, KM, 3, CH, KM), (2, 3, 4, 0, 1))
        full = jnp.zeros((3, CH, NZ, NX, NY), cube.dtype)
        full = full.at[:, :, depth_index, first_index, second_index].set(cube)
        spectral = jnp.fft.ifftn(full, axes=(2, 3, 4), norm="ortho")
        cotangent = to_complex(output_grad[sample])
        bypass = jnp.einsum("oi,kozxy->kizxy", jnp.conj(b_scalar), cotangent)
        columns = []
        for target in range(CH):
            term = 0.0
            for source in range(CH):
                term = term + 1j * jnp.cross(jnp.conj(b_vector[:, source, target])[:, None, None, None], cotangent[:, source], axis=0)
            columns.append(term)
        bypass = bypass + jnp.stack(columns, axis=1)
        summed = spectral + bypass
        outputs.append(jnp.concatenate([jnp.real(summed), jnp.imag(summed)], axis=0).astype(jnp.bfloat16))
    input_grad = jnp.stack(outputs)
    weight_grad = jnp.concatenate([jnp.real(scalar_grad)[:, None], jnp.real(vector_grad), jnp.imag(scalar_grad)[:, None], jnp.imag(vector_grad)], axis=1)
    return input_grad, weight_grad.astype(jnp.float32)
```

```python
import functools

import jax
import jax.numpy as jnp
import ml_dtypes
import numpy as np
from jax import lax
from jax.experimental import pallas as pl
from jax.experimental.pallas import tpu as pltpu
from jax.sharding import PartitionSpec as P

N = 256
KM = 32
PLANES = 2
SLABS = 128
GROUPS = 4
SCALE = 2.0**-12
VMEM = pltpu.VMEM


def frequencies():
    counter = np.arange(KM)
    return np.where(counter < KM // 2, counter, counter - KM)


def circle(positions):
    angles = 2.0 * np.pi * ((positions[:, None] * frequencies()[None, :]) % N) / N
    return np.cos(angles), np.sin(angles)


def split(table):
    high = table.astype(ml_dtypes.bfloat16)
    low = (table - high.astype(np.float64)).astype(ml_dtypes.bfloat16)
    return high, low


def interleave(real, imag):
    rows = real.shape[0]
    both = np.stack([real.reshape(rows, GROUPS, 8), imag.reshape(rows, GROUPS, 8)], axis=2)
    return both.reshape(rows, 2 * KM)


@functools.cache
def tables():
    cos, sin = circle(np.arange(N))
    from_real = np.concatenate(split(interleave(cos, -sin)), axis=1)
    from_imag = np.concatenate(split(interleave(sin, cos)), axis=1)
    forward_y = np.stack([from_real, from_imag])
    forward_x = np.concatenate(split(np.concatenate([cos.T, sin.T], axis=0)), axis=0)
    depth = np.concatenate([cos, sin], axis=1).astype(np.float32) * np.float32(SCALE)
    depth_back = np.concatenate([depth[0::2], depth[1::2]], axis=1)
    to_real = interleave(cos, -sin).T
    to_imag = interleave(sin, cos).T
    high, low = split(np.concatenate([to_real, to_imag], axis=1))
    inverse_y = np.concatenate([high, high, low, np.zeros_like(low)], axis=0)
    high, low = split(np.block([[cos, -sin], [sin, cos]]))
    inverse_x = np.concatenate([high, high, low], axis=1)
    return forward_y, forward_x, depth, depth_back, inverse_y, inverse_x


def dot(left, right):
    return jnp.dot(left, right, preferred_element_type=jnp.float32)


def exact_dot(left, right, dims):
    return lax.dot_general(
        left,
        right,
        (dims, ((), ())),
        precision=lax.Precision.HIGHEST,
        preferred_element_type=jnp.float32,
    )


def lanes(rows):
    return lax.broadcasted_iota(jnp.int32, (rows, 128), 1)


def roll(value, shift):
    shift = shift % 128
    return value if shift == 0 else pltpu.roll(value, shift, 1)


def forward_kernel(saved_ref, grad_ref, table_y_ref, table_x_ref, out_ref):
    plane = pl.program_id(0)
    low_half = lanes(N) < 64
    is_real = (lanes(KM) // 8) % 2 == 0
    slot = lanes(KM) // 16
    modes = []
    for ref in (saved_ref, grad_ref):
        for axis in range(3):
            rows = dot(ref[axis, 0], table_y_ref[0]) + dot(ref[3 + axis, 0], table_y_ref[1])
            rows = rows + roll(rows, 64)
            high = rows.astype(jnp.bfloat16).astype(jnp.float32)
            rows = jnp.where(low_half, high, rows - high).astype(jnp.bfloat16)
            both = dot(table_x_ref[...], rows)
            both = both[:64] + both[64:]
            both = both + roll(both, 64)
            with_cos, with_sin = both[:KM], both[KM:]
            modes.append(with_cos + jnp.where(is_real, roll(with_sin, -8), -roll(with_sin, 8)))
    for group in range(GROUPS):
        gathered = jnp.zeros((KM, 128), jnp.float32)
        for place, value in enumerate(modes):
            gathered = jnp.where(slot == place, roll(value, 16 * (place - group)), gathered)
        out_ref[pl.ds(group * PLANES + plane, KM, stride=GROUPS * PLANES), :] = gathered


def cross_three(left, right):
    return (
        left[1] * right[2] - left[2] * right[1],
        left[2] * right[0] - left[0] * right[2],
        left[0] * right[1] - left[1] * right[0],
    )


def cross_conjugated(left_real, left_imag, right_real, right_imag):
    first = cross_three(left_real, right_real)
    second = cross_three(left_imag, right_imag)
    third = cross_three(left_real, right_imag)
    fourth = cross_three(left_imag, right_real)
    return [a + b for a, b in zip(first, second)], [a - b for a, b in zip(third, fourth)]


def adjoint_product(scalar_real, scalar_imag, vector_real, vector_imag, grad_real, grad_imag):
    cross_real, cross_imag = cross_conjugated(vector_real, vector_imag, grad_real, grad_imag)
    real_part = [
        scalar_real * grad_real[i] + scalar_imag * grad_imag[i] - cross_imag[i] for i in range(3)
    ]
    imag_part = [
        scalar_real * grad_imag[i] - scalar_imag * grad_real[i] + cross_real[i] for i in range(3)
    ]
    return real_part, imag_part


def middle_kernel(planes_ref, weight_ref, depth_ref, back_ref, grad_out_ref, out_ref):
    spectra = exact_dot(planes_ref[...].T, depth_ref[...], ((1,), (0,)))
    with_cos, with_sin = spectra[:, :KM], spectra[:, KM:]
    real, imag = [], []
    for place in range(6):
        at_real, at_imag = slice(16 * place, 16 * place + 8), slice(16 * place + 8, 16 * place + 16)
        real.append(with_cos[at_real] + with_sin[at_imag])
        imag.append(with_cos[at_imag] - with_sin[at_real])
    inputs_real, inputs_imag, grads_real, grads_imag = real[:3], imag[:3], real[3:], imag[3:]
    scalar_real = sum(
        inputs_real[i] * grads_real[i] + inputs_imag[i] * grads_imag[i] for i in range(3)
    )
    scalar_imag = sum(
        inputs_real[i] * grads_imag[i] - inputs_imag[i] * grads_real[i] for i in range(3)
    )
    cross_real, cross_imag = cross_conjugated(inputs_real, inputs_imag, grads_real, grads_imag)
    blades = [scalar_real] + cross_imag + [scalar_imag] + [-entry for entry in cross_real]
    for blade, entry in enumerate(blades):
        grad_out_ref[:, blade, :] = entry
    weight = [weight_ref[:, blade, :] for blade in range(8)]
    mode_real, mode_imag = adjoint_product(
        weight[0], weight[4], weight[1:4], weight[5:8], grads_real, grads_imag
    )
    straight, turned = [], []
    for i in range(3):
        straight += [mode_real[i], mode_imag[i]]
        turned += [-mode_imag[i], mode_real[i]]
    pair = jnp.concatenate(
        [jnp.concatenate(straight, axis=0), jnp.concatenate(turned, axis=0)], axis=1
    )
    pair = jnp.concatenate([pair, jnp.zeros((16, 64), jnp.float32)], axis=0)
    nothing = jnp.zeros((64, 64), jnp.float32)
    blocks = jnp.concatenate(
        [
            jnp.concatenate([pair, nothing], axis=1),
            jnp.concatenate([nothing, pair], axis=1),
        ],
        axis=0,
    )
    out_ref[...] = exact_dot(back_ref[...], blocks, ((1,), (1,)))


def backward_kernel(modes_ref, grad_ref, bypass_ref, table_y_ref, table_x_ref, out_ref, spec_ref):
    plane = pl.program_id(0)
    low_half = lanes(KM) < 64
    slot = lanes(KM) // 16
    groups = []
    for group in range(GROUPS):
        value = modes_ref[pl.ds(group, KM, stride=GROUPS), :]
        groups.append(jnp.where(plane == 0, value, roll(value, 64)))
    left = []
    for axis in range(3):
        gathered = jnp.zeros((KM, 128), jnp.float32)
        for place in range(8):
            gathered = jnp.where(
                slot == place, roll(groups[place % GROUPS], 16 * (place - axis)), gathered
            )
        high = gathered.astype(jnp.bfloat16).astype(jnp.float32)
        first = jnp.where(low_half, high, gathered - high)
        second = jnp.where(low_half, high, 0.0)
        left.append(jnp.concatenate([first, second], axis=1).astype(jnp.bfloat16))
    along_y = dot(jnp.concatenate(left, axis=0), table_y_ref[...])
    for axis in range(3):
        rows = along_y[axis * KM : (axis + 1) * KM]
        rows = jnp.concatenate([rows[:, :N], rows[:, N:]], axis=0)
        high = rows.astype(jnp.bfloat16)
        low = (rows - high.astype(jnp.float32)).astype(jnp.bfloat16)
        spec_ref[axis] = dot(table_x_ref[...], jnp.concatenate([high, low, high], axis=0))
    weight = [bypass_ref[blade] for blade in range(8)]
    step = 16

    def chunk(index, carry):
        start = pl.multiple_of(index * step, step)
        here = pl.ds(start, step)
        fields = [grad_ref[entry, 0, here, :].astype(jnp.float32) for entry in range(6)]
        real, imag = adjoint_product(
            weight[0], weight[4], weight[1:4], weight[5:8], fields[:3], fields[3:]
        )
        for axis in range(3):
            total = spec_ref[axis, here, :] + real[axis]
            out_ref[axis, 0, here, :] = total.astype(jnp.bfloat16)
            there = pl.ds(pl.multiple_of(start + N, step), step)
            total = spec_ref[axis, there, :] + imag[axis]
            out_ref[3 + axis, 0, here, :] = total.astype(jnp.bfloat16)
        return carry

    lax.fori_loop(0, N // step, chunk, 0)


def whole(shape):
    return pl.BlockSpec(shape, lambda *_: (0,) * len(shape))


FIELD = pl.BlockSpec((6, 1, N, N), lambda plane: (0, plane, 0, 0))
PARAMS = pltpu.CompilerParams(vmem_limit_bytes=32 * 1024 * 1024)


def forward(saved, grad, table_y, table_x, interpret=False):
    return pl.pallas_call(
        forward_kernel,
        grid=(PLANES,),
        in_specs=[FIELD, FIELD, whole((2, N, 128)), whole((128, N))],
        out_specs=whole((SLABS * PLANES, 128)),
        out_shape=jax.ShapeDtypeStruct((SLABS * PLANES, 128), jnp.float32),
        compiler_params=PARAMS,
        interpret=interpret,
        name="to_plane_modes",
    )(saved, grad, table_y, table_x)


def middle(planes, weight, depth, back, interpret=False):
    return pl.pallas_call(
        middle_kernel,
        out_shape=(
            jax.ShapeDtypeStruct((8, 8, KM), jnp.float32),
            jax.ShapeDtypeStruct((SLABS, 128), jnp.float32),
        ),
        compiler_params=PARAMS,
        interpret=interpret,
        name="mode_products",
    )(planes, weight, depth, back)


def backward(modes, grad, bypass, table_y, table_x, interpret=False):
    return pl.pallas_call(
        backward_kernel,
        grid=(PLANES,),
        in_specs=[
            whole((SLABS, 128)),
            FIELD,
            pl.BlockSpec(memory_space=pltpu.SMEM),
            whole((N, 2 * N)),
            whole((2 * N, 192)),
        ],
        out_specs=FIELD,
        out_shape=jax.ShapeDtypeStruct((6, PLANES, N, N), jnp.bfloat16),
        scratch_shapes=[VMEM((3, 2 * N, N), jnp.float32)],
        compiler_params=PARAMS,
        interpret=interpret,
        name="to_input_grad",
    )(modes, grad, bypass, table_y, table_x)


def shards(saved_input, output_grad, spectral_weight, bypass_weight):
    forward_y, forward_x, depth, depth_back, inverse_y, inverse_x = tables()
    saved = saved_input.reshape(6, PLANES, N, N)
    grad = output_grad.reshape(6, PLANES, N, N)
    modes = forward(saved, grad, forward_y, forward_x)
    rows = lax.all_to_all(modes.reshape(SLABS, PLANES, 128), "slab", 0, 0, tiled=True)
    local_grad, mode_grads = middle(
        rows.reshape(SLABS * PLANES, 128), spectral_weight.reshape(8, 8, KM), depth, depth_back
    )
    back = lax.all_to_all(mode_grads.reshape(SLABS, 1, 128), "slab", 0, 0, tiled=True)
    weight_grad = jnp.sum(lax.all_gather(local_grad, "rep"), axis=0)
    input_grad = backward(
        back.reshape(SLABS, 128), grad, bypass_weight.reshape(8), inverse_y, inverse_x
    )
    return (
        input_grad.reshape(1, 6, 1, PLANES, N, N),
        weight_grad.reshape(8, 8, 1, 1, KM),
    )


def solution(mesh):
    field = P("rep", None, None, "slab", None, None)
    weight = P("slab", None, None, None, None)
    return jax.shard_map(
        shards,
        mesh=mesh,
        in_specs=(field, field, weight, P()),
        out_specs=(field, weight),
        check_vma=False,
    )
```

```python
import functools

import jax
import jax.numpy as jnp
import ml_dtypes
import numpy as np
from jax import lax
from jax.experimental import pallas as pl
from jax.experimental.pallas import tpu as pltpu
from jax.sharding import PartitionSpec as P

N = 256
KM = 32
PLANES = 2
SLABS = 128
GROUPS = 4
SCALE = 2.0**-12


def frequencies():
    counter = np.arange(KM)
    return np.where(counter < KM // 2, counter, counter - KM)


def circle(positions):
    angles = 2.0 * np.pi * ((positions[:, None] * frequencies()[None, :]) % N) / N
    return np.cos(angles), np.sin(angles)


def split(table):
    high = table.astype(ml_dtypes.bfloat16)
    low = (table - high.astype(np.float64)).astype(ml_dtypes.bfloat16)
    return high, low


def interleave(real, imag):
    rows = real.shape[0]
    both = np.stack([real.reshape(rows, GROUPS, 8), imag.reshape(rows, GROUPS, 8)], axis=2)
    return both.reshape(rows, 2 * KM)


@functools.cache
def tables():
    cos, sin = circle(np.arange(N))
    from_real = np.concatenate(split(interleave(cos, -sin)), axis=1)
    from_imag = np.concatenate(split(interleave(sin, cos)), axis=1)
    forward_y = np.stack([from_real, from_imag])
    forward_x = np.concatenate(split(np.concatenate([cos.T, sin.T], axis=0)), axis=0)
    depth = np.concatenate([cos, sin], axis=1) * SCALE
    high, low = split(np.concatenate([depth[0::2], depth[1::2]], axis=1))
    depth_back = np.concatenate([high, high, low], axis=1)
    depth = np.concatenate(split(depth), axis=1)
    to_real = interleave(cos, -sin).T
    to_imag = interleave(sin, cos).T
    high, low = split(np.concatenate([to_real, to_imag], axis=1))
    inverse_y = np.concatenate([high, high, low, np.zeros_like(low)], axis=0)
    high, low = split(np.block([[cos, -sin], [sin, cos]]))
    inverse_x = np.concatenate([high, high, low], axis=1)
    return forward_y, forward_x, depth, depth_back, inverse_y, inverse_x


def dot(left, right):
    return jnp.dot(left, right, preferred_element_type=jnp.float32)


def lanes(rows):
    return lax.broadcasted_iota(jnp.int32, (rows, 128), 1)


def roll(value, shift):
    shift = shift % 128
    return value if shift == 0 else pltpu.roll(value, shift, 1)


def forward_kernel(saved_ref, grad_ref, far_y_ref, far_x_ref, out_ref, fields, table_y, table_x, rows_ref, sems):
    copies = [
        pltpu.make_async_copy(far_y_ref, table_y, sems.at[0]),
        pltpu.make_async_copy(far_x_ref, table_x, sems.at[1]),
    ]
    for field, ref in enumerate((saved_ref, grad_ref)):
        for entry in range(6):
            copies.append(
                pltpu.make_async_copy(
                    ref.at[entry], fields.at[field, entry], sems.at[2 + 6 * field + entry]
                )
            )
    for copy in copies:
        copy.start()
    for copy in copies:
        copy.wait()
    is_real = (lanes(KM) // 8) % 2 == 0
    slot = lanes(KM) // 16
    places = [(field, axis) for field in range(2) for axis in range(3)]
    for place, (field, axis) in enumerate(places):
        real = fields[field, axis].reshape(PLANES * N, N)
        imag = fields[field, 3 + axis].reshape(PLANES * N, N)
        rows = dot(real, table_y[0]) + dot(imag, table_y[1])
        high = rows.astype(jnp.bfloat16)
        rows_ref[place, :, :128] = high
        rows_ref[place, :, 128:] = (rows - high.astype(jnp.float32)).astype(jnp.bfloat16)
    for plane in range(PLANES):
        modes = []
        for place in range(6):
            both = dot(table_x[...], rows_ref[place, plane * N : (plane + 1) * N, :])
            both = both[:64] + both[64:]
            both = both[:, :128] + both[:, 128:]
            both = both + roll(both, 64)
            with_cos, with_sin = both[:KM], both[KM:]
            modes.append(with_cos + jnp.where(is_real, roll(with_sin, -8), -roll(with_sin, 8)))
        for group in range(GROUPS):
            gathered = jnp.zeros((KM, 128), jnp.float32)
            for place, value in enumerate(modes):
                gathered = jnp.where(slot == place, roll(value, 16 * (place - group)), gathered)
            out_ref[pl.ds(group * PLANES + plane, KM, stride=GROUPS * PLANES), :] = gathered


def cross_three(left, right):
    return (
        left[1] * right[2] - left[2] * right[1],
        left[2] * right[0] - left[0] * right[2],
        left[0] * right[1] - left[1] * right[0],
    )


def cross_conjugated(left_real, left_imag, right_real, right_imag):
    first = cross_three(left_real, right_real)
    second = cross_three(left_imag, right_imag)
    third = cross_three(left_real, right_imag)
    fourth = cross_three(left_imag, right_real)
    return [a + b for a, b in zip(first, second)], [a - b for a, b in zip(third, fourth)]


def adjoint_product(scalar_real, scalar_imag, vector_real, vector_imag, grad_real, grad_imag):
    cross_real, cross_imag = cross_conjugated(vector_real, vector_imag, grad_real, grad_imag)
    real_part = [
        scalar_real * grad_real[i] + scalar_imag * grad_imag[i] - cross_imag[i] for i in range(3)
    ]
    imag_part = [
        scalar_real * grad_imag[i] - scalar_imag * grad_real[i] + cross_real[i] for i in range(3)
    ]
    return real_part, imag_part


def middle_kernel(planes_ref, weight_ref, depth_ref, back_ref, grad_out_ref, out_ref):
    planes = planes_ref[...].T
    high = planes.astype(jnp.bfloat16)
    low = (planes - high.astype(jnp.float32)).astype(jnp.bfloat16)
    spectra = dot(high, depth_ref[...]) + dot(low, depth_ref[...])
    spectra = spectra + roll(spectra, 64)
    with_cos, with_sin = spectra[:, :KM], spectra[:, KM:64]
    real, imag = [], []
    for place in range(6):
        at_real, at_imag = slice(16 * place, 16 * place + 8), slice(16 * place + 8, 16 * place + 16)
        real.append(with_cos[at_real] + with_sin[at_imag])
        imag.append(with_cos[at_imag] - with_sin[at_real])
    inputs_real, inputs_imag, grads_real, grads_imag = real[:3], imag[:3], real[3:], imag[3:]
    scalar_real = sum(
        inputs_real[i] * grads_real[i] + inputs_imag[i] * grads_imag[i] for i in range(3)
    )
    scalar_imag = sum(
        inputs_real[i] * grads_imag[i] - inputs_imag[i] * grads_real[i] for i in range(3)
    )
    cross_real, cross_imag = cross_conjugated(inputs_real, inputs_imag, grads_real, grads_imag)
    blades = [scalar_real] + cross_imag + [scalar_imag] + [-entry for entry in cross_real]
    for blade, entry in enumerate(blades):
        grad_out_ref[:, blade, :] = entry
    weight = [weight_ref[:, blade, :] for blade in range(8)]
    mode_real, mode_imag = adjoint_product(
        weight[0], weight[4], weight[1:4], weight[5:8], grads_real, grads_imag
    )
    straight, turned = [], []
    for i in range(3):
        straight += [mode_real[i], mode_imag[i]]
        turned += [-mode_imag[i], mode_real[i]]
    pair = jnp.concatenate(
        [jnp.concatenate(straight, axis=0), jnp.concatenate(turned, axis=0)], axis=1
    )
    pair = jnp.concatenate([pair, jnp.zeros((16, 64), jnp.float32)], axis=0)
    nothing = jnp.zeros((64, 64), jnp.float32)
    blocks = jnp.concatenate(
        [
            jnp.concatenate([pair, nothing], axis=1),
            jnp.concatenate([nothing, pair], axis=1),
        ],
        axis=0,
    )
    high = blocks.astype(jnp.bfloat16)
    low = (blocks - high.astype(jnp.float32)).astype(jnp.bfloat16)
    out_ref[...] = lax.dot_general(
        back_ref[...],
        jnp.concatenate([high, low, high], axis=1),
        (((1,), (1,)), ((), ())),
        preferred_element_type=jnp.float32,
    )


def bypass_kernel(grad_ref, bypass_ref, out_ref, field, sems):
    copies = [
        pltpu.make_async_copy(grad_ref.at[:, plane], field.at[:, plane], sems.at[plane])
        for plane in range(PLANES)
    ]
    for copy in copies:
        copy.start()
    weight = [bypass_ref[blade] for blade in range(8)]
    step = 32
    for plane in range(PLANES):
        copies[plane].wait()

        def chunk(index, carry):
            here = pl.ds(pl.multiple_of(index * step, step), step)
            fields = [field[entry, plane, here, :].astype(jnp.float32) for entry in range(6)]
            real, imag = adjoint_product(
                weight[0], weight[4], weight[1:4], weight[5:8], fields[:3], fields[3:]
            )
            for axis in range(3):
                out_ref[axis, plane, here, :] = real[axis]
                out_ref[3 + axis, plane, here, :] = imag[axis]
            return carry

        lax.fori_loop(0, N // step, chunk, 0)

def backward_kernel(
    modes_ref, bypass_ref, far_y_ref, far_x_ref, out_ref, table_y, table_x, total_ref, near_sems, sems
):
    fetch_y = pltpu.make_async_copy(far_y_ref, table_y, near_sems.at[0])
    fetch_x = pltpu.make_async_copy(far_x_ref, table_x, near_sems.at[1])
    fetch_y.start()
    fetch_x.start()
    low_half = lanes(KM) < 64
    slot = lanes(KM) // 16
    groups = [modes_ref[pl.ds(group, KM, stride=GROUPS), :] for group in range(GROUPS)]
    left = []
    for plane in range(PLANES):
        for axis in range(3):
            gathered = jnp.zeros((KM, 128), jnp.float32)
            for place in range(8):
                value = roll(groups[place % GROUPS], 16 * (place - axis) - 64 * plane)
                gathered = jnp.where(slot == place, value, gathered)
            high = gathered.astype(jnp.bfloat16).astype(jnp.float32)
            first = jnp.where(low_half, high, gathered - high)
            second = jnp.where(low_half, high, 0.0)
            left.append(jnp.concatenate([first, second], axis=1).astype(jnp.bfloat16))
    left = jnp.concatenate(left, axis=0)
    fetch_y.wait()
    fetch_x.wait()
    along_y = dot(left, table_y[...])
    right = []
    for part in range(3 * PLANES):
        rows = along_y[part * KM : (part + 1) * KM]
        rows = jnp.concatenate([rows[:, :N], rows[:, N:]], axis=0)
        high = rows.astype(jnp.bfloat16)
        low = (rows - high.astype(jnp.float32)).astype(jnp.bfloat16)
        right.append(jnp.concatenate([high, low, high], axis=0))
    copies = []
    for part in range(3 * PLANES):
        plane, axis = divmod(part, 3)
        spectral = dot(table_x[...], right[part])
        for entry, rows in ((axis, spectral[:N]), (3 + axis, spectral[N:])):
            total = rows + bypass_ref[entry, plane]
            total_ref[entry, plane] = total.astype(jnp.bfloat16)
        for entry in (axis, 3 + axis):
            copies.append(
                pltpu.make_async_copy(
                    total_ref.at[entry, plane], out_ref.at[entry, plane], sems.at[entry, plane]
                )
            )
            copies[-1].start()
    for copy in copies:
        copy.wait()


NEAR = pl.BlockSpec(memory_space=pltpu.VMEM)
FAR = pl.BlockSpec(memory_space=pltpu.HBM)


def params(mebibytes):
    return pltpu.CompilerParams(vmem_limit_bytes=mebibytes * 1024 * 1024)


def cost(flops, moved):
    return pl.CostEstimate(flops=flops, bytes_accessed=moved, transcendentals=0)


def forward(saved, grad, table_y, table_x, interpret=False):
    return pl.pallas_call(
        forward_kernel,
        in_specs=[FAR] * 4,
        out_specs=NEAR,
        out_shape=jax.ShapeDtypeStruct((SLABS * PLANES, 128), jnp.float32),
        scratch_shapes=[
            pltpu.VMEM((2, 6, PLANES, N, N), jnp.bfloat16),
            pltpu.VMEM((2, N, 128), jnp.bfloat16),
            pltpu.VMEM((128, N), jnp.bfloat16),
            pltpu.VMEM((6, PLANES * N, N), jnp.bfloat16),
            pltpu.SemaphoreType.DMA((14,)),
        ],
        compiler_params=params(24),
        cost_estimate=cost(10**9, 3 * 2**20),
        interpret=interpret,
        name="to_plane_modes",
    )(saved, grad, table_y, table_x)


def middle(planes, weight, depth, back, interpret=False):
    return pl.pallas_call(
        middle_kernel,
        in_specs=[NEAR] * 4,
        out_specs=(NEAR, NEAR),
        out_shape=(
            jax.ShapeDtypeStruct((8, 8, KM), jnp.float32),
            jax.ShapeDtypeStruct((SLABS, 128), jnp.float32),
        ),
        compiler_params=params(16),
        cost_estimate=cost(10**8, 2**20),
        interpret=interpret,
        name="mode_products",
    )(planes, weight, depth, back)


def bypass(grad, weight, interpret=False):
    return pl.pallas_call(
        bypass_kernel,
        in_specs=[FAR, pl.BlockSpec(memory_space=pltpu.SMEM)],
        out_specs=NEAR,
        out_shape=jax.ShapeDtypeStruct((6, PLANES, N, N), jnp.float32),
        scratch_shapes=[
            pltpu.VMEM((6, PLANES, N, N), jnp.bfloat16),
            pltpu.SemaphoreType.DMA((PLANES,)),
        ],
        compiler_params=params(16),
        cost_estimate=cost(10**8, 6 * 2**20),
        interpret=interpret,
        name="bypass",
    )(grad, weight)


def backward(modes, bypassed, table_y, table_x, interpret=False):
    return pl.pallas_call(
        backward_kernel,
        in_specs=[NEAR, NEAR, FAR, FAR],
        out_specs=FAR,
        out_shape=jax.ShapeDtypeStruct((6, PLANES, N, N), jnp.bfloat16),
        scratch_shapes=[
            pltpu.VMEM((N, 2 * N), jnp.bfloat16),
            pltpu.VMEM((2 * N, 192), jnp.bfloat16),
            pltpu.VMEM((6, PLANES, N, N), jnp.bfloat16),
            pltpu.SemaphoreType.DMA((2,)),
            pltpu.SemaphoreType.DMA((6, PLANES)),
        ],
        compiler_params=params(24),
        cost_estimate=cost(10**9, 6 * 2**20),
        interpret=interpret,
        name="to_input_grad",
    )(modes, bypassed, table_y, table_x)


def shards(saved_input, output_grad, spectral_weight, bypass_weight):
    forward_y, forward_x, depth, depth_back, inverse_y, inverse_x = tables()
    saved = saved_input.reshape(6, PLANES, N, N)
    grad = output_grad.reshape(6, PLANES, N, N)
    far = functools.partial(pltpu.with_memory_space_constraint, memory_space=pltpu.HBM)
    modes = forward(far(saved), far(grad), far(forward_y), far(forward_x))
    rows = lax.all_to_all(modes.reshape(SLABS, PLANES, 128), "slab", 0, 0, tiled=True)
    local_grad, mode_grads = middle(
        rows.reshape(SLABS * PLANES, 128), spectral_weight.reshape(8, 8, KM), depth, depth_back
    )
    back = lax.all_to_all(mode_grads.reshape(SLABS, 1, 128), "slab", 0, 0, tiled=True)
    local_grad, later = lax.optimization_barrier((local_grad, grad))
    bypassed = bypass(far(later), bypass_weight.reshape(8))
    weight_grad = jnp.sum(lax.all_gather(local_grad, "rep"), axis=0)
    input_grad = backward(back.reshape(SLABS, 128), bypassed, far(inverse_y), far(inverse_x))
    return (
        input_grad.reshape(1, 6, 1, PLANES, N, N),
        weight_grad.reshape(8, 8, 1, 1, KM),
    )


def solution(mesh):
    field = P("rep", None, None, "slab", None, None)
    weight = P("slab", None, None, None, None)
    return jax.shard_map(
        shards,
        mesh=mesh,
        in_specs=(field, field, weight, P()),
        out_specs=(field, weight),
        check_vma=False,
    )
```

```python
import functools

import jax
import jax.numpy as jnp
import ml_dtypes
import numpy as np
from jax import lax
from jax.experimental import pallas as pl
from jax.experimental.pallas import tpu as pltpu
from jax.sharding import PartitionSpec as P

N = 256
KM = 32
PLANES = 2
SLABS = 128
GROUPS = 4
SCALE = 2.0**-12


def frequencies():
    counter = np.arange(KM)
    return np.where(counter < KM // 2, counter, counter - KM)


def circle(positions):
    angles = 2.0 * np.pi * ((positions[:, None] * frequencies()[None, :]) % N) / N
    return np.cos(angles), np.sin(angles)


def split(table):
    high = table.astype(ml_dtypes.bfloat16)
    low = (table - high.astype(np.float64)).astype(ml_dtypes.bfloat16)
    return high, low


def interleave(real, imag):
    rows = real.shape[0]
    both = np.stack([real.reshape(rows, GROUPS, 8), imag.reshape(rows, GROUPS, 8)], axis=2)
    return both.reshape(rows, 2 * KM)


@functools.cache
def tables():
    cos, sin = circle(np.arange(N))
    from_real = np.concatenate(split(interleave(cos, -sin)), axis=1)
    from_imag = np.concatenate(split(interleave(sin, cos)), axis=1)
    forward_y = np.stack([from_real, from_imag])
    forward_x = np.concatenate(split(np.concatenate([cos.T, sin.T], axis=0)), axis=0)
    depth = np.concatenate([cos, sin], axis=1) * SCALE
    high, low = split(np.concatenate([depth[0::2], depth[1::2]], axis=1))
    depth_back = np.concatenate([high, high, low], axis=1)
    depth = np.concatenate(split(depth), axis=1)
    to_real = interleave(cos, -sin).T
    to_imag = interleave(sin, cos).T
    inverse = np.zeros((N, 2 * N), ml_dtypes.bfloat16)
    inverse[:128] = np.concatenate(split(np.concatenate([to_real, to_imag], axis=1)), axis=0)
    inverse_x = np.concatenate(split(np.block([[cos, -sin], [sin, cos]])), axis=1)
    for block in range(4):
        place = slice(128 * block, 128 * block + 128)
        inverse[128:, place] = inverse_x[place]
    return forward_y, forward_x, depth, depth_back, inverse


def dot(left, right):
    return jnp.dot(left, right, preferred_element_type=jnp.float32)


def lanes(rows):
    return lax.broadcasted_iota(jnp.int32, (rows, 128), 1)


def roll(value, shift):
    shift = shift % 128
    return value if shift == 0 else pltpu.roll(value, shift, 1)


def forward_kernel(saved_ref, grad_ref, far_y_ref, far_x_ref, out_ref, fields, table_y, table_x, rows_ref, sems):
    copies = [
        pltpu.make_async_copy(far_y_ref, table_y, sems.at[0]),
        pltpu.make_async_copy(far_x_ref, table_x, sems.at[1]),
    ]
    for field, ref in enumerate((saved_ref, grad_ref)):
        for entry in range(6):
            copies.append(
                pltpu.make_async_copy(
                    ref.at[entry], fields.at[field, entry], sems.at[2 + 6 * field + entry]
                )
            )
    for copy in copies:
        copy.start()
    for copy in copies:
        copy.wait()
    is_real = (lanes(KM) // 8) % 2 == 0
    slot = lanes(KM) // 16
    places = [(field, axis) for field in range(2) for axis in range(3)]
    for place, (field, axis) in enumerate(places):
        real = fields[field, axis].reshape(PLANES * N, N)
        imag = fields[field, 3 + axis].reshape(PLANES * N, N)
        rows = dot(real, table_y[0]) + dot(imag, table_y[1])
        high = rows.astype(jnp.bfloat16)
        rows_ref[place, :, :128] = high
        rows_ref[place, :, 128:] = (rows - high.astype(jnp.float32)).astype(jnp.bfloat16)
    for plane in range(PLANES):
        modes = []
        for place in range(6):
            both = dot(table_x[...], rows_ref[place, plane * N : (plane + 1) * N, :])
            both = both[:64] + both[64:]
            both = both[:, :128] + both[:, 128:]
            both = both + roll(both, 64)
            with_cos, with_sin = both[:KM], both[KM:]
            modes.append(with_cos + jnp.where(is_real, roll(with_sin, -8), -roll(with_sin, 8)))
        for group in range(GROUPS):
            gathered = jnp.zeros((KM, 128), jnp.float32)
            for place, value in enumerate(modes):
                gathered = jnp.where(slot == place, roll(value, 16 * (place - group)), gathered)
            out_ref[pl.ds(group * PLANES + plane, KM, stride=GROUPS * PLANES), :] = gathered


def cross_three(left, right):
    return (
        left[1] * right[2] - left[2] * right[1],
        left[2] * right[0] - left[0] * right[2],
        left[0] * right[1] - left[1] * right[0],
    )


def cross_conjugated(left_real, left_imag, right_real, right_imag):
    first = cross_three(left_real, right_real)
    second = cross_three(left_imag, right_imag)
    third = cross_three(left_real, right_imag)
    fourth = cross_three(left_imag, right_real)
    return [a + b for a, b in zip(first, second)], [a - b for a, b in zip(third, fourth)]


def adjoint_product(scalar_real, scalar_imag, vector_real, vector_imag, grad_real, grad_imag):
    cross_real, cross_imag = cross_conjugated(vector_real, vector_imag, grad_real, grad_imag)
    real_part = [
        scalar_real * grad_real[i] + scalar_imag * grad_imag[i] - cross_imag[i] for i in range(3)
    ]
    imag_part = [
        scalar_real * grad_imag[i] - scalar_imag * grad_real[i] + cross_real[i] for i in range(3)
    ]
    return real_part, imag_part


def middle_kernel(planes_ref, weight_ref, depth_ref, back_ref, grad_out_ref, out_ref):
    planes = planes_ref[...].T
    high = planes.astype(jnp.bfloat16)
    low = (planes - high.astype(jnp.float32)).astype(jnp.bfloat16)
    spectra = dot(high, depth_ref[...]) + dot(low, depth_ref[...])
    spectra = spectra + roll(spectra, 64)
    with_cos, with_sin = spectra[:, :KM], spectra[:, KM:64]
    real, imag = [], []
    for place in range(6):
        at_real, at_imag = slice(16 * place, 16 * place + 8), slice(16 * place + 8, 16 * place + 16)
        real.append(with_cos[at_real] + with_sin[at_imag])
        imag.append(with_cos[at_imag] - with_sin[at_real])
    inputs_real, inputs_imag, grads_real, grads_imag = real[:3], imag[:3], real[3:], imag[3:]
    scalar_real = sum(
        inputs_real[i] * grads_real[i] + inputs_imag[i] * grads_imag[i] for i in range(3)
    )
    scalar_imag = sum(
        inputs_real[i] * grads_imag[i] - inputs_imag[i] * grads_real[i] for i in range(3)
    )
    cross_real, cross_imag = cross_conjugated(inputs_real, inputs_imag, grads_real, grads_imag)
    blades = [scalar_real] + cross_imag + [scalar_imag] + [-entry for entry in cross_real]
    for blade, entry in enumerate(blades):
        grad_out_ref[:, blade, :] = entry
    weight = [weight_ref[:, blade, :] for blade in range(8)]
    mode_real, mode_imag = adjoint_product(
        weight[0], weight[4], weight[1:4], weight[5:8], grads_real, grads_imag
    )
    straight, turned = [], []
    for i in range(3):
        straight += [mode_real[i], mode_imag[i]]
        turned += [-mode_imag[i], mode_real[i]]
    pair = jnp.concatenate(
        [jnp.concatenate(straight, axis=0), jnp.concatenate(turned, axis=0)], axis=1
    )
    pair = jnp.concatenate([pair, jnp.zeros((16, 64), jnp.float32)], axis=0)
    nothing = jnp.zeros((64, 64), jnp.float32)
    blocks = jnp.concatenate(
        [
            jnp.concatenate([pair, nothing], axis=1),
            jnp.concatenate([nothing, pair], axis=1),
        ],
        axis=0,
    )
    high = blocks.astype(jnp.bfloat16)
    low = (blocks - high.astype(jnp.float32)).astype(jnp.bfloat16)
    out_ref[...] = lax.dot_general(
        back_ref[...],
        jnp.concatenate([high, low, high], axis=1),
        (((1,), (1,)), ((), ())),
        preferred_element_type=jnp.float32,
    )


def bypass_kernel(
    grad_ref, bypass_ref, parts_ref, out_ref, sum_ref, field, sems
):
    copies = [
        pltpu.make_async_copy(grad_ref.at[:, plane], field.at[:, plane], sems.at[plane])
        for plane in range(PLANES)
    ]
    for copy in copies:
        copy.start()
    sum_ref[...] = (parts_ref[0] + parts_ref[1]) + (parts_ref[2] + parts_ref[3])
    weight = [bypass_ref[blade] for blade in range(8)]
    step = 32
    for plane in range(PLANES):
        copies[plane].wait()

        def chunk(index, carry):
            here = pl.ds(pl.multiple_of(index * step, step), step)
            fields = [field[entry, plane, here, :].astype(jnp.float32) for entry in range(6)]
            real, imag = adjoint_product(
                weight[0], weight[4], weight[1:4], weight[5:8], fields[:3], fields[3:]
            )
            for axis in range(3):
                out_ref[axis, plane, here, :] = real[axis]
                out_ref[3 + axis, plane, here, :] = imag[axis]
            return carry

        lax.fori_loop(0, N // step, chunk, 0)

def backward_kernel(modes_ref, bypass_ref, table_ref, out_ref, total_ref, sems):
    high, low = table_ref[:64, :], table_ref[64:128, :]
    table_y = jnp.concatenate([high, high, low, low], axis=0)
    table_x = jnp.concatenate(
        [table_ref[128:, 128 * block : 128 * block + 128] for block in range(4)], axis=0
    )
    table_x = jnp.concatenate([table_x, table_x], axis=1)
    low_half = lanes(KM) < 64
    slot = lanes(KM) // 16
    groups = [modes_ref[pl.ds(group, KM, stride=GROUPS), :] for group in range(GROUPS)]
    left = []
    for plane in range(PLANES):
        for axis in range(3):
            gathered = jnp.zeros((KM, 128), jnp.float32)
            for place in range(8):
                value = roll(groups[place % GROUPS], 16 * (place - axis) - 64 * plane)
                gathered = jnp.where(slot == place, value, gathered)
            high = gathered.astype(jnp.bfloat16).astype(jnp.float32)
            both = jnp.where(low_half, high, gathered - high).astype(jnp.bfloat16)
            left.append(jnp.concatenate([both, both], axis=1))
    along_y = dot(jnp.concatenate(left, axis=0), table_y)
    right = []
    for part in range(3 * PLANES):
        rows = along_y[part * KM : (part + 1) * KM]
        rows = jnp.concatenate([rows[:, :N], rows[:, N:]], axis=0)
        high = rows.astype(jnp.bfloat16)
        low = (rows - high.astype(jnp.float32)).astype(jnp.bfloat16)
        right.append(jnp.concatenate([high, high, low, low], axis=0))
    copies = []
    for part in range(3 * PLANES):
        plane, axis = divmod(part, 3)
        spectral = dot(table_x, right[part])
        for entry, rows in ((axis, spectral[:N]), (3 + axis, spectral[N:])):
            total = rows + bypass_ref[entry, plane]
            total_ref[entry, plane] = total.astype(jnp.bfloat16)
        for entry in (axis, 3 + axis):
            copies.append(
                pltpu.make_async_copy(
                    total_ref.at[entry, plane], out_ref.at[entry, plane], sems.at[entry, plane]
                )
            )
            copies[-1].start()
    for copy in copies:
        copy.wait()


NEAR = pl.BlockSpec(memory_space=pltpu.VMEM)
FAR = pl.BlockSpec(memory_space=pltpu.HBM)


def params(mebibytes):
    return pltpu.CompilerParams(vmem_limit_bytes=mebibytes * 1024 * 1024)


def cost(flops, moved):
    return pl.CostEstimate(flops=flops, bytes_accessed=moved, transcendentals=0)


def forward(saved, grad, table_y, table_x, interpret=False):
    return pl.pallas_call(
        forward_kernel,
        in_specs=[FAR] * 4,
        out_specs=NEAR,
        out_shape=jax.ShapeDtypeStruct((SLABS * PLANES, 128), jnp.float32),
        scratch_shapes=[
            pltpu.VMEM((2, 6, PLANES, N, N), jnp.bfloat16),
            pltpu.VMEM((2, N, 128), jnp.bfloat16),
            pltpu.VMEM((128, N), jnp.bfloat16),
            pltpu.VMEM((6, PLANES * N, N), jnp.bfloat16),
            pltpu.SemaphoreType.DMA((14,)),
        ],
        compiler_params=params(24),
        cost_estimate=cost(10**9, 3 * 2**20),
        interpret=interpret,
        name="to_plane_modes",
    )(saved, grad, table_y, table_x)


def middle(planes, weight, depth, back, interpret=False):
    return pl.pallas_call(
        middle_kernel,
        in_specs=[NEAR] * 4,
        out_specs=(NEAR, NEAR),
        out_shape=(
            jax.ShapeDtypeStruct((8, 8, KM), jnp.float32),
            jax.ShapeDtypeStruct((SLABS, 128), jnp.float32),
        ),
        compiler_params=params(16),
        cost_estimate=cost(10**8, 2**20),
        interpret=interpret,
        name="mode_products",
    )(planes, weight, depth, back)


def bypass(grad, weight, parts, interpret=False):
    return pl.pallas_call(
        bypass_kernel,
        in_specs=[FAR, pl.BlockSpec(memory_space=pltpu.SMEM), NEAR],
        out_specs=(NEAR, NEAR),
        out_shape=(
            jax.ShapeDtypeStruct((6, PLANES, N, N), jnp.float32),
            jax.ShapeDtypeStruct(parts.shape[1:], parts.dtype),
        ),
        scratch_shapes=[
            pltpu.VMEM((6, PLANES, N, N), jnp.bfloat16),
            pltpu.SemaphoreType.DMA((PLANES,)),
        ],
        compiler_params=params(16),
        cost_estimate=cost(10**8, 6 * 2**20),
        interpret=interpret,
        name="bypass",
    )(grad, weight, parts)


def backward(modes, bypassed, table, interpret=False):
    return pl.pallas_call(
        backward_kernel,
        in_specs=[NEAR] * 3,
        out_specs=FAR,
        out_shape=jax.ShapeDtypeStruct((6, PLANES, N, N), jnp.bfloat16),
        scratch_shapes=[
            pltpu.VMEM((6, PLANES, N, N), jnp.bfloat16),
            pltpu.SemaphoreType.DMA((6, PLANES)),
        ],
        compiler_params=params(16),
        cost_estimate=cost(10**8, 2**20),
        interpret=interpret,
        name="to_input_grad",
    )(modes, bypassed, table)


def shards(saved_input, output_grad, spectral_weight, bypass_weight):
    forward_y, forward_x, depth, depth_back, inverse = tables()
    saved = saved_input.reshape(6, PLANES, N, N)
    grad = output_grad.reshape(6, PLANES, N, N)
    far = functools.partial(pltpu.with_memory_space_constraint, memory_space=pltpu.HBM)
    modes = forward(far(saved), far(grad), far(forward_y), far(forward_x))
    rows = lax.all_to_all(modes.reshape(SLABS, PLANES, 128), "slab", 0, 0, tiled=True)
    local_grad, mode_grads = middle(
        rows.reshape(SLABS * PLANES, 128), spectral_weight.reshape(8, 8, KM), depth, depth_back
    )
    back = lax.all_to_all(mode_grads.reshape(SLABS, 1, 128), "slab", 0, 0, tiled=True)
    bypassed, weight_grad = bypass(
        far(grad), bypass_weight.reshape(8), lax.all_gather(local_grad, "rep")
    )
    input_grad = backward(back.reshape(SLABS, 128), bypassed, inverse)
    return (
        input_grad.reshape(1, 6, 1, PLANES, N, N),
        weight_grad.reshape(8, 8, 1, 1, KM),
    )


def solution(mesh):
    field = P("rep", None, None, "slab", None, None)
    weight = P("slab", None, None, None, None)
    return jax.shard_map(
        shards,
        mesh=mesh,
        in_specs=(field, field, weight, P()),
        out_specs=(field, weight),
        check_vma=False,
    )
```

```python
import functools

import jax
import jax.numpy as jnp
import ml_dtypes
import numpy as np
from jax import lax
from jax.experimental import pallas as pl
from jax.experimental.pallas import tpu as pltpu
from jax.sharding import PartitionSpec as P

N = 256
KM = 32
PLANES = 2
SLABS = 128
GROUPS = 4
SCALE = 2.0**-12


def frequencies():
    counter = np.arange(KM)
    return np.where(counter < KM // 2, counter, counter - KM)


def circle(positions):
    angles = 2.0 * np.pi * ((positions[:, None] * frequencies()[None, :]) % N) / N
    return np.cos(angles), np.sin(angles)


def split(table):
    high = table.astype(ml_dtypes.bfloat16)
    low = (table - high.astype(np.float64)).astype(ml_dtypes.bfloat16)
    return high, low


def interleave(real, imag):
    rows = real.shape[0]
    both = np.stack([real.reshape(rows, GROUPS, 8), imag.reshape(rows, GROUPS, 8)], axis=2)
    return both.reshape(rows, 2 * KM)


@functools.cache
def tables():
    cos, sin = circle(np.arange(N))
    from_real = np.concatenate(split(interleave(cos, -sin)), axis=1)
    from_imag = np.concatenate(split(interleave(sin, cos)), axis=1)
    forward_y = np.stack([from_real, from_imag])
    forward_x = np.concatenate(split(np.concatenate([cos.T, sin.T], axis=0)), axis=0)
    depth = np.concatenate([cos, sin], axis=1) * SCALE
    high, low = split(np.concatenate([depth[0::2], depth[1::2]], axis=1))
    depth_back = np.concatenate([high, high, low], axis=1)
    depth = np.concatenate(split(depth), axis=1)
    to_real = interleave(cos, -sin).T
    to_imag = interleave(sin, cos).T
    inverse = np.zeros((N, 2 * N), ml_dtypes.bfloat16)
    inverse[:128] = np.concatenate(split(np.concatenate([to_real, to_imag], axis=1)), axis=0)
    inverse_x = np.concatenate(split(np.block([[cos, -sin], [sin, cos]])), axis=1)
    for block in range(4):
        place = slice(128 * block, 128 * block + 128)
        inverse[128:, place] = inverse_x[place]
    return forward_y, forward_x, depth, depth_back, inverse


def dot(left, right):
    return jnp.dot(left, right, preferred_element_type=jnp.float32)


def lanes(rows):
    return lax.broadcasted_iota(jnp.int32, (rows, 128), 1)


def roll(value, shift):
    shift = shift % 128
    return value if shift == 0 else pltpu.roll(value, shift, 1)


def forward_kernel(saved_ref, grad_ref, far_y_ref, far_x_ref, out_ref, fields, table_y, table_x, rows_ref, sems):
    near_y = pltpu.make_async_copy(far_y_ref, table_y, sems.at[0])
    near_x = pltpu.make_async_copy(far_x_ref, table_x, sems.at[1])
    near_saved = pltpu.make_async_copy(saved_ref, fields.at[0], sems.at[2])
    near_grad = pltpu.make_async_copy(grad_ref, fields.at[1], sems.at[3])
    near_y.start()
    near_x.start()
    for entry in range(6):
        pltpu.make_async_copy(saved_ref.at[entry], fields.at[0, entry], sems.at[2]).start()
    near_grad.start()
    near_y.wait()
    near_x.wait()
    is_real = (lanes(KM) // 8) % 2 == 0
    slot = lanes(KM) // 16
    for field, whole_field in enumerate((near_saved, near_grad)):
        whole_field.wait()
        for axis in range(3):
            place = 3 * field + axis
            real = fields[field, axis].reshape(PLANES * N, N)
            imag = fields[field, 3 + axis].reshape(PLANES * N, N)
            rows = dot(real, table_y[0]) + dot(imag, table_y[1])
            high = rows.astype(jnp.bfloat16)
            rows_ref[place, :, :128] = high
            rows_ref[place, :, 128:] = (rows - high.astype(jnp.float32)).astype(jnp.bfloat16)
    for plane in range(PLANES):
        modes = []
        for place in range(6):
            both = dot(table_x[...], rows_ref[place, plane * N : (plane + 1) * N, :])
            both = both[:64] + both[64:]
            both = both[:, :128] + both[:, 128:]
            both = both + roll(both, 64)
            with_cos, with_sin = both[:KM], both[KM:]
            modes.append(with_cos + jnp.where(is_real, roll(with_sin, -8), -roll(with_sin, 8)))
        for group in range(GROUPS):
            gathered = jnp.zeros((KM, 128), jnp.float32)
            for place, value in enumerate(modes):
                gathered = jnp.where(slot == place, roll(value, 16 * (place - group)), gathered)
            out_ref[pl.ds(group * PLANES + plane, KM, stride=GROUPS * PLANES), :] = gathered


def cross_three(left, right):
    return (
        left[1] * right[2] - left[2] * right[1],
        left[2] * right[0] - left[0] * right[2],
        left[0] * right[1] - left[1] * right[0],
    )


def cross_conjugated(left_real, left_imag, right_real, right_imag):
    first = cross_three(left_real, right_real)
    second = cross_three(left_imag, right_imag)
    third = cross_three(left_real, right_imag)
    fourth = cross_three(left_imag, right_real)
    return [a + b for a, b in zip(first, second)], [a - b for a, b in zip(third, fourth)]


def adjoint_product(scalar_real, scalar_imag, vector_real, vector_imag, grad_real, grad_imag):
    cross_real, cross_imag = cross_conjugated(vector_real, vector_imag, grad_real, grad_imag)
    real_part = [
        scalar_real * grad_real[i] + scalar_imag * grad_imag[i] - cross_imag[i] for i in range(3)
    ]
    imag_part = [
        scalar_real * grad_imag[i] - scalar_imag * grad_real[i] + cross_real[i] for i in range(3)
    ]
    return real_part, imag_part


def middle_kernel(planes_ref, weight_ref, depth_ref, back_ref, grad_out_ref, out_ref):
    planes = planes_ref[...].T
    high = planes.astype(jnp.bfloat16)
    low = (planes - high.astype(jnp.float32)).astype(jnp.bfloat16)
    spectra = dot(high, depth_ref[...]) + dot(low, depth_ref[...])
    spectra = spectra + roll(spectra, 64)
    with_cos, with_sin = spectra[:, :KM], spectra[:, KM:64]
    real, imag = [], []
    for place in range(6):
        at_real, at_imag = slice(16 * place, 16 * place + 8), slice(16 * place + 8, 16 * place + 16)
        real.append(with_cos[at_real] + with_sin[at_imag])
        imag.append(with_cos[at_imag] - with_sin[at_real])
    inputs_real, inputs_imag, grads_real, grads_imag = real[:3], imag[:3], real[3:], imag[3:]
    scalar_real = sum(
        inputs_real[i] * grads_real[i] + inputs_imag[i] * grads_imag[i] for i in range(3)
    )
    scalar_imag = sum(
        inputs_real[i] * grads_imag[i] - inputs_imag[i] * grads_real[i] for i in range(3)
    )
    cross_real, cross_imag = cross_conjugated(inputs_real, inputs_imag, grads_real, grads_imag)
    blades = [scalar_real] + cross_imag + [scalar_imag] + [-entry for entry in cross_real]
    for blade, entry in enumerate(blades):
        grad_out_ref[:, blade, :] = entry
    weight = [weight_ref[:, blade, :] for blade in range(8)]
    mode_real, mode_imag = adjoint_product(
        weight[0], weight[4], weight[1:4], weight[5:8], grads_real, grads_imag
    )
    straight, turned = [], []
    for i in range(3):
        straight += [mode_real[i], mode_imag[i]]
        turned += [-mode_imag[i], mode_real[i]]
    pair = jnp.concatenate(
        [jnp.concatenate(straight, axis=0), jnp.concatenate(turned, axis=0)], axis=1
    )
    pair = jnp.concatenate([pair, jnp.zeros((16, 64), jnp.float32)], axis=0)
    nothing = jnp.zeros((64, 64), jnp.float32)
    blocks = jnp.concatenate(
        [
            jnp.concatenate([pair, nothing], axis=1),
            jnp.concatenate([nothing, pair], axis=1),
        ],
        axis=0,
    )
    high = blocks.astype(jnp.bfloat16)
    low = (blocks - high.astype(jnp.float32)).astype(jnp.bfloat16)
    out_ref[...] = lax.dot_general(
        back_ref[...],
        jnp.concatenate([high, low, high], axis=1),
        (((1,), (1,)), ((), ())),
        preferred_element_type=jnp.float32,
    )


def bypass_kernel(
    grad_ref, bypass_ref, parts_ref, out_ref, sum_ref, field, sems
):
    copies = [
        pltpu.make_async_copy(grad_ref.at[:, plane], field.at[:, plane], sems.at[plane])
        for plane in range(PLANES)
    ]
    for copy in copies:
        copy.start()
    sum_ref[...] = (parts_ref[0] + parts_ref[1]) + (parts_ref[2] + parts_ref[3])
    weight = [bypass_ref[blade] for blade in range(8)]
    step = 32
    for plane in range(PLANES):
        copies[plane].wait()

        def chunk(index, carry):
            here = pl.ds(pl.multiple_of(index * step, step), step)
            fields = [field[entry, plane, here, :].astype(jnp.float32) for entry in range(6)]
            real, imag = adjoint_product(
                weight[0], weight[4], weight[1:4], weight[5:8], fields[:3], fields[3:]
            )
            for axis in range(3):
                out_ref[axis, plane, here, :] = real[axis]
                out_ref[3 + axis, plane, here, :] = imag[axis]
            return carry

        lax.fori_loop(0, N // step, chunk, 0)

def backward_kernel(modes_ref, bypass_ref, table_ref, out_ref, total_ref, sem):
    high, low = table_ref[:64, :], table_ref[64:128, :]
    table_y = jnp.concatenate([high, high, low, low], axis=0)
    table_x = jnp.concatenate(
        [table_ref[128:, 128 * block : 128 * block + 128] for block in range(4)], axis=0
    )
    table_x = jnp.concatenate([table_x, table_x], axis=1)
    low_half = lanes(KM) < 64
    slot = lanes(KM) // 16
    groups = [modes_ref[pl.ds(group, KM, stride=GROUPS), :] for group in range(GROUPS)]
    left = []
    for plane in range(PLANES):
        for axis in range(3):
            gathered = jnp.zeros((KM, 128), jnp.float32)
            for place in range(8):
                value = roll(groups[place % GROUPS], 16 * (place - axis) - 64 * plane)
                gathered = jnp.where(slot == place, value, gathered)
            high = gathered.astype(jnp.bfloat16).astype(jnp.float32)
            both = jnp.where(low_half, high, gathered - high).astype(jnp.bfloat16)
            left.append(jnp.concatenate([both, both], axis=1))
    along_y = dot(jnp.concatenate(left, axis=0), table_y)
    right = []
    for part in range(3 * PLANES):
        rows = along_y[part * KM : (part + 1) * KM]
        rows = jnp.concatenate([rows[:, :N], rows[:, N:]], axis=0)
        high = rows.astype(jnp.bfloat16)
        low = (rows - high.astype(jnp.float32)).astype(jnp.bfloat16)
        right.append(jnp.concatenate([high, high, low, low], axis=0))
    for part in range(3 * PLANES):
        plane, axis = divmod(part, 3)
        spectral = dot(table_x, right[part])
        for entry, rows in ((axis, spectral[:N]), (3 + axis, spectral[N:])):
            total = rows + bypass_ref[entry, plane]
            total_ref[entry, plane] = total.astype(jnp.bfloat16)
        for entry in (axis, 3 + axis):
            pltpu.make_async_copy(
                total_ref.at[entry, plane], out_ref.at[entry, plane], sem
            ).start()
    pltpu.make_async_copy(total_ref, out_ref, sem).wait()


NEAR = pl.BlockSpec(memory_space=pltpu.VMEM)
FAR = pl.BlockSpec(memory_space=pltpu.HBM)


def params(mebibytes):
    return pltpu.CompilerParams(vmem_limit_bytes=mebibytes * 1024 * 1024)


def cost(flops, moved):
    return pl.CostEstimate(flops=flops, bytes_accessed=moved, transcendentals=0)


def forward(saved, grad, table_y, table_x, interpret=False):
    return pl.pallas_call(
        forward_kernel,
        in_specs=[FAR] * 4,
        out_specs=NEAR,
        out_shape=jax.ShapeDtypeStruct((SLABS * PLANES, 128), jnp.float32),
        scratch_shapes=[
            pltpu.VMEM((2, 6, PLANES, N, N), jnp.bfloat16),
            pltpu.VMEM((2, N, 128), jnp.bfloat16),
            pltpu.VMEM((128, N), jnp.bfloat16),
            pltpu.VMEM((6, PLANES * N, N), jnp.bfloat16),
            pltpu.SemaphoreType.DMA((4,)),
        ],
        compiler_params=params(24),
        cost_estimate=cost(10**9, 3 * 2**20),
        interpret=interpret,
        name="to_plane_modes",
    )(saved, grad, table_y, table_x)


def middle(planes, weight, depth, back, interpret=False):
    return pl.pallas_call(
        middle_kernel,
        in_specs=[NEAR] * 4,
        out_specs=(NEAR, NEAR),
        out_shape=(
            jax.ShapeDtypeStruct((8, 8, KM), jnp.float32),
            jax.ShapeDtypeStruct((SLABS, 128), jnp.float32),
        ),
        compiler_params=params(16),
        cost_estimate=cost(10**8, 2**20),
        interpret=interpret,
        name="mode_products",
    )(planes, weight, depth, back)


def bypass(grad, weight, parts, interpret=False):
    return pl.pallas_call(
        bypass_kernel,
        in_specs=[FAR, pl.BlockSpec(memory_space=pltpu.SMEM), NEAR],
        out_specs=(NEAR, NEAR),
        out_shape=(
            jax.ShapeDtypeStruct((6, PLANES, N, N), jnp.float32),
            jax.ShapeDtypeStruct(parts.shape[1:], parts.dtype),
        ),
        scratch_shapes=[
            pltpu.VMEM((6, PLANES, N, N), jnp.bfloat16),
            pltpu.SemaphoreType.DMA((PLANES,)),
        ],
        compiler_params=params(16),
        cost_estimate=cost(10**8, 6 * 2**20),
        interpret=interpret,
        name="bypass",
    )(grad, weight, parts)


def backward(modes, bypassed, table, interpret=False):
    return pl.pallas_call(
        backward_kernel,
        in_specs=[NEAR] * 3,
        out_specs=FAR,
        out_shape=jax.ShapeDtypeStruct((6, PLANES, N, N), jnp.bfloat16),
        scratch_shapes=[
            pltpu.VMEM((6, PLANES, N, N), jnp.bfloat16),
            pltpu.SemaphoreType.DMA(()),
        ],
        compiler_params=params(16),
        cost_estimate=cost(10**8, 2**20),
        interpret=interpret,
        name="to_input_grad",
    )(modes, bypassed, table)


def shards(saved_input, output_grad, spectral_weight, bypass_weight):
    forward_y, forward_x, depth, depth_back, inverse = tables()
    saved = saved_input.reshape(6, PLANES, N, N)
    grad = output_grad.reshape(6, PLANES, N, N)
    far = functools.partial(pltpu.with_memory_space_constraint, memory_space=pltpu.HBM)
    modes = forward(far(saved), far(grad), far(forward_y), far(forward_x))
    rows = lax.all_to_all(modes.reshape(SLABS, PLANES, 128), "slab", 0, 0, tiled=True)
    local_grad, mode_grads = middle(
        rows.reshape(SLABS * PLANES, 128), spectral_weight.reshape(8, 8, KM), depth, depth_back
    )
    back = lax.all_to_all(mode_grads.reshape(SLABS, 1, 128), "slab", 0, 0, tiled=True)
    bypassed, weight_grad = bypass(
        far(grad), bypass_weight.reshape(8), lax.all_gather(local_grad, "rep")
    )
    input_grad = backward(back.reshape(SLABS, 128), bypassed, inverse)
    return (
        input_grad.reshape(1, 6, 1, PLANES, N, N),
        weight_grad.reshape(8, 8, 1, 1, KM),
    )


def solution(mesh):
    field = P("rep", None, None, "slab", None, None)
    weight = P("slab", None, None, None, None)
    return jax.shard_map(
        shards,
        mesh=mesh,
        in_specs=(field, field, weight, P()),
        out_specs=(field, weight),
        check_vma=False,
    )
```

```python
import functools

import jax
import jax.numpy as jnp
import ml_dtypes
import numpy as np
from jax import lax
from jax.experimental import pallas as pl
from jax.experimental.pallas import tpu as pltpu
from jax.sharding import PartitionSpec as P

N = 256
KM = 32
PLANES = 2
SLABS = 128
GROUPS = 4
SCALE = 2.0**-12


def frequencies():
    counter = np.arange(KM)
    return np.where(counter < KM // 2, counter, counter - KM)


def circle(positions):
    angles = 2.0 * np.pi * ((positions[:, None] * frequencies()[None, :]) % N) / N
    return np.cos(angles), np.sin(angles)


def split(table):
    high = table.astype(ml_dtypes.bfloat16)
    low = (table - high.astype(np.float64)).astype(ml_dtypes.bfloat16)
    return high, low


def interleave(real, imag):
    rows = real.shape[0]
    both = np.stack([real.reshape(rows, GROUPS, 8), imag.reshape(rows, GROUPS, 8)], axis=2)
    return both.reshape(rows, 2 * KM)


@functools.cache
def tables():
    cos, sin = circle(np.arange(N))
    from_real = np.concatenate(split(interleave(cos, -sin)), axis=1)
    from_imag = np.concatenate(split(interleave(sin, cos)), axis=1)
    forward_x = np.concatenate(split(np.concatenate([cos.T, sin.T], axis=0)), axis=0)
    forward_table = np.stack([from_real, from_imag, np.concatenate([forward_x[:, :128], forward_x[:, 128:]])])
    depth = np.concatenate([cos, sin], axis=1) * SCALE
    high, low = split(np.concatenate([depth[0::2], depth[1::2]], axis=1))
    depth_back = np.concatenate([high, high, low], axis=1)
    depth = np.concatenate(split(depth), axis=1)
    to_real = interleave(cos, -sin).T
    to_imag = interleave(sin, cos).T
    inverse = np.zeros((N, 2 * N), ml_dtypes.bfloat16)
    inverse[:128] = np.concatenate(split(np.concatenate([to_real, to_imag], axis=1)), axis=0)
    inverse_x = np.concatenate(split(np.block([[cos, -sin], [sin, cos]])), axis=1)
    for block in range(4):
        place = slice(128 * block, 128 * block + 128)
        inverse[128:, place] = inverse_x[place]
    return forward_table, depth, depth_back, inverse


def dot(left, right):
    return jnp.dot(left, right, preferred_element_type=jnp.float32)


def lanes(rows):
    return lax.broadcasted_iota(jnp.int32, (rows, 128), 1)


def roll(value, shift):
    shift = shift % 128
    return value if shift == 0 else pltpu.roll(value, shift, 1)


def forward_kernel(saved_ref, grad_ref, far_ref, out_ref, fields, table_ref, rows_ref, sems):
    near_table = pltpu.make_async_copy(far_ref, table_ref, sems.at[0])
    near_saved = pltpu.make_async_copy(saved_ref, fields.at[0], sems.at[1])
    near_grad = pltpu.make_async_copy(grad_ref, fields.at[1], sems.at[2])
    near_table.start()
    for entry in range(6):
        pltpu.make_async_copy(saved_ref.at[entry], fields.at[0, entry], sems.at[1]).start()
    near_grad.start()
    near_table.wait()
    table_x = jnp.concatenate([table_ref[2, :128], table_ref[2, 128:]], axis=1)
    is_real = (lanes(KM) // 8) % 2 == 0
    slot = lanes(KM) // 16
    for field, whole_field in enumerate((near_saved, near_grad)):
        whole_field.wait()
        for axis in range(3):
            place = 3 * field + axis
            real = fields[field, axis].reshape(PLANES * N, N)
            imag = fields[field, 3 + axis].reshape(PLANES * N, N)
            rows = dot(real, table_ref[0]) + dot(imag, table_ref[1])
            high = rows.astype(jnp.bfloat16)
            rows_ref[place, :, :128] = high
            rows_ref[place, :, 128:] = (rows - high.astype(jnp.float32)).astype(jnp.bfloat16)
    for plane in range(PLANES):
        modes = []
        for place in range(6):
            both = dot(table_x, rows_ref[place, plane * N : (plane + 1) * N, :])
            both = both[:64] + both[64:]
            both = both[:, :128] + both[:, 128:]
            both = both + roll(both, 64)
            with_cos, with_sin = both[:KM], both[KM:]
            modes.append(with_cos + jnp.where(is_real, roll(with_sin, -8), -roll(with_sin, 8)))
        for group in range(GROUPS):
            gathered = jnp.zeros((KM, 128), jnp.float32)
            for place, value in enumerate(modes):
                gathered = jnp.where(slot == place, roll(value, 16 * (place - group)), gathered)
            out_ref[pl.ds(group * PLANES + plane, KM, stride=GROUPS * PLANES), :] = gathered


def cross_three(left, right):
    return (
        left[1] * right[2] - left[2] * right[1],
        left[2] * right[0] - left[0] * right[2],
        left[0] * right[1] - left[1] * right[0],
    )


def cross_conjugated(left_real, left_imag, right_real, right_imag):
    first = cross_three(left_real, right_real)
    second = cross_three(left_imag, right_imag)
    third = cross_three(left_real, right_imag)
    fourth = cross_three(left_imag, right_real)
    return [a + b for a, b in zip(first, second)], [a - b for a, b in zip(third, fourth)]


def adjoint_product(scalar_real, scalar_imag, vector_real, vector_imag, grad_real, grad_imag):
    cross_real, cross_imag = cross_conjugated(vector_real, vector_imag, grad_real, grad_imag)
    real_part = [
        scalar_real * grad_real[i] + scalar_imag * grad_imag[i] - cross_imag[i] for i in range(3)
    ]
    imag_part = [
        scalar_real * grad_imag[i] - scalar_imag * grad_real[i] + cross_real[i] for i in range(3)
    ]
    return real_part, imag_part


def middle_kernel(planes_ref, weight_ref, depth_ref, back_ref, grad_out_ref, out_ref):
    planes = planes_ref[...].T
    high = planes.astype(jnp.bfloat16)
    low = (planes - high.astype(jnp.float32)).astype(jnp.bfloat16)
    spectra = dot(high, depth_ref[...]) + dot(low, depth_ref[...])
    spectra = spectra + roll(spectra, 64)
    with_cos, with_sin = spectra[:, :KM], spectra[:, KM:64]
    real, imag = [], []
    for place in range(6):
        at_real, at_imag = slice(16 * place, 16 * place + 8), slice(16 * place + 8, 16 * place + 16)
        real.append(with_cos[at_real] + with_sin[at_imag])
        imag.append(with_cos[at_imag] - with_sin[at_real])
    inputs_real, inputs_imag, grads_real, grads_imag = real[:3], imag[:3], real[3:], imag[3:]
    scalar_real = sum(
        inputs_real[i] * grads_real[i] + inputs_imag[i] * grads_imag[i] for i in range(3)
    )
    scalar_imag = sum(
        inputs_real[i] * grads_imag[i] - inputs_imag[i] * grads_real[i] for i in range(3)
    )
    cross_real, cross_imag = cross_conjugated(inputs_real, inputs_imag, grads_real, grads_imag)
    blades = [scalar_real] + cross_imag + [scalar_imag] + [-entry for entry in cross_real]
    for blade, entry in enumerate(blades):
        grad_out_ref[:, blade, :] = entry
    weight = [weight_ref[:, blade, :] for blade in range(8)]
    mode_real, mode_imag = adjoint_product(
        weight[0], weight[4], weight[1:4], weight[5:8], grads_real, grads_imag
    )
    straight, turned = [], []
    for i in range(3):
        straight += [mode_real[i], mode_imag[i]]
        turned += [-mode_imag[i], mode_real[i]]
    pair = jnp.concatenate(
        [jnp.concatenate(straight, axis=0), jnp.concatenate(turned, axis=0)], axis=1
    )
    pair = jnp.concatenate([pair, jnp.zeros((16, 64), jnp.float32)], axis=0)
    nothing = jnp.zeros((64, 64), jnp.float32)
    blocks = jnp.concatenate(
        [
            jnp.concatenate([pair, nothing], axis=1),
            jnp.concatenate([nothing, pair], axis=1),
        ],
        axis=0,
    )
    high = blocks.astype(jnp.bfloat16)
    low = (blocks - high.astype(jnp.float32)).astype(jnp.bfloat16)
    out_ref[...] = lax.dot_general(
        back_ref[...],
        jnp.concatenate([high, low, high], axis=1),
        (((1,), (1,)), ((), ())),
        preferred_element_type=jnp.float32,
    )


def bypass_kernel(
    grad_ref, bypass_ref, parts_ref, out_ref, sum_ref, field, sems
):
    copies = [
        pltpu.make_async_copy(grad_ref.at[:, plane], field.at[:, plane], sems.at[plane])
        for plane in range(PLANES)
    ]
    for copy in copies:
        copy.start()
    sum_ref[...] = (parts_ref[0] + parts_ref[1]) + (parts_ref[2] + parts_ref[3])
    weight = [bypass_ref[blade] for blade in range(8)]
    step = 32
    for plane in range(PLANES):
        copies[plane].wait()

        def chunk(index, carry):
            here = pl.ds(pl.multiple_of(index * step, step), step)
            fields = [field[entry, plane, here, :].astype(jnp.float32) for entry in range(6)]
            real, imag = adjoint_product(
                weight[0], weight[4], weight[1:4], weight[5:8], fields[:3], fields[3:]
            )
            for axis in range(3):
                out_ref[axis, plane, here, :] = real[axis]
                out_ref[3 + axis, plane, here, :] = imag[axis]
            return carry

        lax.fori_loop(0, N // step, chunk, 0)

def backward_kernel(modes_ref, bypass_ref, table_ref, out_ref, total_ref, sem):
    high, low = table_ref[:64, :], table_ref[64:128, :]
    table_y = jnp.concatenate([high, high, low, low], axis=0)
    table_x = jnp.concatenate(
        [table_ref[128:, 128 * block : 128 * block + 128] for block in range(4)], axis=0
    )
    table_x = jnp.concatenate([table_x, table_x], axis=1)
    low_half = lanes(KM) < 64
    slot = lanes(KM) // 16
    groups = [modes_ref[pl.ds(group, KM, stride=GROUPS), :] for group in range(GROUPS)]
    left = []
    for plane in range(PLANES):
        for axis in range(3):
            gathered = jnp.zeros((KM, 128), jnp.float32)
            for place in range(8):
                value = roll(groups[place % GROUPS], 16 * (place - axis) - 64 * plane)
                gathered = jnp.where(slot == place, value, gathered)
            high = gathered.astype(jnp.bfloat16).astype(jnp.float32)
            both = jnp.where(low_half, high, gathered - high).astype(jnp.bfloat16)
            left.append(jnp.concatenate([both, both], axis=1))
    along_y = dot(jnp.concatenate(left, axis=0), table_y)
    right = []
    for part in range(3 * PLANES):
        rows = along_y[part * KM : (part + 1) * KM]
        rows = jnp.concatenate([rows[:, :N], rows[:, N:]], axis=0)
        high = rows.astype(jnp.bfloat16)
        low = (rows - high.astype(jnp.float32)).astype(jnp.bfloat16)
        right.append(jnp.concatenate([high, high, low, low], axis=0))
    for part in range(3 * PLANES):
        plane, axis = divmod(part, 3)
        spectral = dot(table_x, right[part])
        for entry, rows in ((axis, spectral[:N]), (3 + axis, spectral[N:])):
            total = rows + bypass_ref[entry, plane]
            total_ref[entry, plane] = total.astype(jnp.bfloat16)
        for entry in (axis, 3 + axis):
            pltpu.make_async_copy(
                total_ref.at[entry, plane], out_ref.at[entry, plane], sem
            ).start()
    pltpu.make_async_copy(total_ref, out_ref, sem).wait()


NEAR = pl.BlockSpec(memory_space=pltpu.VMEM)
FAR = pl.BlockSpec(memory_space=pltpu.HBM)


def params(mebibytes):
    return pltpu.CompilerParams(vmem_limit_bytes=mebibytes * 1024 * 1024)


def cost(flops, moved):
    return pl.CostEstimate(flops=flops, bytes_accessed=moved, transcendentals=0)


def forward(saved, grad, table, interpret=False):
    return pl.pallas_call(
        forward_kernel,
        in_specs=[FAR] * 3,
        out_specs=NEAR,
        out_shape=jax.ShapeDtypeStruct((SLABS * PLANES, 128), jnp.float32),
        scratch_shapes=[
            pltpu.VMEM((2, 6, PLANES, N, N), jnp.bfloat16),
            pltpu.VMEM((3, N, 128), jnp.bfloat16),
            pltpu.VMEM((6, PLANES * N, N), jnp.bfloat16),
            pltpu.SemaphoreType.DMA((3,)),
        ],
        compiler_params=params(24),
        cost_estimate=cost(10**9, 3 * 2**20),
        interpret=interpret,
        name="to_plane_modes",
    )(saved, grad, table)


def middle(planes, weight, depth, back, interpret=False):
    return pl.pallas_call(
        middle_kernel,
        in_specs=[NEAR] * 4,
        out_specs=(NEAR, NEAR),
        out_shape=(
            jax.ShapeDtypeStruct((8, 8, KM), jnp.float32),
            jax.ShapeDtypeStruct((SLABS, 128), jnp.float32),
        ),
        compiler_params=params(16),
        cost_estimate=cost(10**8, 2**20),
        interpret=interpret,
        name="mode_products",
    )(planes, weight, depth, back)


def bypass(grad, weight, parts, interpret=False):
    return pl.pallas_call(
        bypass_kernel,
        in_specs=[FAR, pl.BlockSpec(memory_space=pltpu.SMEM), NEAR],
        out_specs=(NEAR, NEAR),
        out_shape=(
            jax.ShapeDtypeStruct((6, PLANES, N, N), jnp.float32),
            jax.ShapeDtypeStruct(parts.shape[1:], parts.dtype),
        ),
        scratch_shapes=[
            pltpu.VMEM((6, PLANES, N, N), jnp.bfloat16),
            pltpu.SemaphoreType.DMA((PLANES,)),
        ],
        compiler_params=params(16),
        cost_estimate=cost(10**8, 6 * 2**20),
        interpret=interpret,
        name="bypass",
    )(grad, weight, parts)


def backward(modes, bypassed, table, interpret=False):
    return pl.pallas_call(
        backward_kernel,
        in_specs=[NEAR] * 3,
        out_specs=FAR,
        out_shape=jax.ShapeDtypeStruct((6, PLANES, N, N), jnp.bfloat16),
        scratch_shapes=[
            pltpu.VMEM((6, PLANES, N, N), jnp.bfloat16),
            pltpu.SemaphoreType.DMA(()),
        ],
        compiler_params=params(16),
        cost_estimate=cost(10**8, 2**20),
        interpret=interpret,
        name="to_input_grad",
    )(modes, bypassed, table)


def shards(saved_input, output_grad, spectral_weight, bypass_weight):
    forward_table, depth, depth_back, inverse = tables()
    saved = saved_input.reshape(6, PLANES, N, N)
    grad = output_grad.reshape(6, PLANES, N, N)
    far = functools.partial(pltpu.with_memory_space_constraint, memory_space=pltpu.HBM)
    modes = forward(far(saved), far(grad), far(forward_table))
    rows = lax.all_to_all(modes.reshape(SLABS, PLANES, 128), "slab", 0, 0, tiled=True)
    local_grad, mode_grads = middle(
        rows.reshape(SLABS * PLANES, 128), spectral_weight.reshape(8, 8, KM), depth, depth_back
    )
    back = lax.all_to_all(mode_grads.reshape(SLABS, 1, 128), "slab", 0, 0, tiled=True)
    bypassed, weight_grad = bypass(
        far(grad), bypass_weight.reshape(8), lax.all_gather(local_grad, "rep")
    )
    input_grad = backward(back.reshape(SLABS, 128), bypassed, inverse)
    return (
        input_grad.reshape(1, 6, 1, PLANES, N, N),
        weight_grad.reshape(8, 8, 1, 1, KM),
    )


def solution(mesh):
    field = P("rep", None, None, "slab", None, None)
    weight = P("slab", None, None, None, None)
    return jax.shard_map(
        shards,
        mesh=mesh,
        in_specs=(field, field, weight, P()),
        out_specs=(field, weight),
        check_vma=False,
    )
```
